32 devices in a mesh: tile: 8 (over y, x, core), sub: 4 (over z).
Axes of the slice: x: 2, y: 2, z: 4, core: 2. Of those that a mesh axis runs over, the one named last changes fastest.
Arguments:
- source: bfloat16 [131072, 128], P(('tile', 'sub')), may hold values from -6 to 6
- fetch_blocks: int32 [2, 32, 32], P(None, ('tile', 'sub')), may hold values from -1 to 63, as said below
- pixel_cells: int32 [4, 2560, 256], P(None, ('tile', 'sub')), may hold values from 0 to 4095, as said below
- pixel_weights: float32 [4, 2560, 256], P(None, ('tile', 'sub')), may hold values from 0.1 to 0.5
- seam_flip: int32 [8], replicated, may hold values from 0 to 1, as said below
- encode_weight: bfloat16 [128, 64], replicated, may hold values from -0.5 to 0.5
- encode_bias: float32 [64], replicated, may hold values from -3 to 3
- first_kernel: bfloat16 [3, 3, 64, 64], replicated, may hold values from -0.25 to 0.25
- first_bias: float32 [64], replicated, may hold values from -3 to 3
- second_kernel: bfloat16 [3, 3, 64, 64], replicated, may hold values from -0.25 to 0.25
- second_bias: float32 [64], replicated, may hold values from -3 to 3
Outputs:
- features: bfloat16 [64, 2560, 256], P(None, ('tile', 'sub'))
The draws below stay inside these ranges and needn't reach their ends.
Inputs may be any that keep to these rules, and one draw needn't show every extreme that they name: fetch_blocks[c, d, q] is the block among device q's 64 source blocks that device d requests in slot c, or -1 for an empty slot; the live slots of a pair come first and name distinct blocks; every device has some live slot, and in every draw some device fills all 2 slots from every device. `pixel_cells`: an entry f of a pixel on device d names cell f % 64 of the block that d requests in slot f // (32 * 64) from device (f // 64) % 32, and that slot is never empty. `seam_flip`: both values occur in every draw.
All inputs are finite; a program needn't handle non-finite values.
Results may differ from the reference program's by a relative error of at most 0.0053.
Values may be sent and summed in bfloat16 or wider, within the bound.
A program may use at most 128 MiB of HBM per device.

```python
import jax
import jax.numpy as jnp
from jax import lax

V = 128
CH = 64
KP = 4
SB = 64
CAP = 2
SBLK = 64
SR = 80
TC = 256
TILES = 8
TILE_ROWS = 320
ROWS = 2560
NSRC = 131072
DEVICES = 32


def request_plan(key):
    subkeys = jax.random.split(key, 5)
    devices = jnp.arange(DEVICES, dtype=jnp.int32)
    counts = jax.random.randint(subkeys[0], (DEVICES, DEVICES), 0, CAP)
    polar_rows = jax.random.randint(subkeys[1], (DEVICES,), 0, 8) == 0
    polar_rows = polar_rows | (devices == jax.random.randint(subkeys[2], (), 0, DEVICES))
    counts = jnp.where(polar_rows[:, None], CAP, counts)
    chosen = jax.random.randint(subkeys[3], (DEVICES,), 0, DEVICES)
    counts = jnp.where(devices[None, :] == chosen[:, None], jnp.maximum(counts, 1), counts)
    starts = jax.random.randint(subkeys[4], (DEVICES, DEVICES), 0, SBLK)
    slot_numbers = jnp.arange(CAP, dtype=jnp.int32)[:, None, None]
    present = slot_numbers < counts[None]
    blocks = jnp.where(present, (starts[None] + slot_numbers) % SBLK, -1)
    return (blocks.astype(jnp.int32), present)


def draw_fetch_blocks(key, part):
    blocks, present = request_plan(key)
    return blocks


def draw_pixel_cells(key, part):
    blocks, present = request_plan(key)
    key = jax.random.fold_in(key, 7)
    subkeys = jax.random.split(key, 2)
    by_device = jnp.transpose(present, (1, 0, 2)).reshape(DEVICES, CAP * DEVICES).astype(jnp.int32)
    positions = jnp.argsort(1 - by_device, axis=1, stable=True).astype(jnp.int32)
    counts = jnp.sum(by_device, axis=1)
    device_rows = jnp.arange(ROWS, dtype=jnp.int32) // SR
    picked = jax.random.randint(subkeys[0], (KP, ROWS, TC), 0, counts[device_rows][None, :, None])
    slot_index = positions[device_rows[None, :, None], picked]
    inner_cell = jax.random.randint(subkeys[1], (KP, ROWS, TC), 0, SB)
    return (slot_index * SB + inner_cell).astype(jnp.int32)


def draw_seam_flip(key, part):
    key = jax.random.fold_in(key, 11)
    subkeys = jax.random.split(key, 2)
    flips = jax.random.randint(subkeys[0], (TILES,), 0, 2)
    shuffled = jax.random.permutation(subkeys[1], TILES)
    positions = jnp.arange(TILES, dtype=jnp.int32)
    flips = jnp.where(positions == shuffled[0], 1, jnp.where(positions == shuffled[1], 0, flips))
    return flips.astype(jnp.int32)


def shard_levels(own_key, dims, cuts, low, top_value):
    loudness, own = 1.0, jax.random.fold_in(own_key, 6)
    for position, parts in cuts:
        draws = jnp.exp(jax.random.uniform(jax.random.fold_in(own, position), (parts,), jnp.float32, low / len(cuts), top_value / len(cuts)))
        loudness = loudness * jnp.repeat(draws, dims[position] // parts).reshape([-1 if axis == position else 1 for axis in range(len(dims))])
    return loudness


def centred(rng, shape, width, limit, pieces=(), kind=jnp.bfloat16):
    drawn = jax.random.normal(rng, shape, jnp.float32) * width
    if len(pieces) > 0:
        drawn = shard_levels(rng, shape, pieces, -0.22, 0.18) * drawn
    return jnp.clip(drawn, min=-limit, max=limit).astype(kind)


def setup_inputs(seed: int = 0) -> dict:
    key_list = jax.random.split(jax.random.key(seed), 12)
    source = centred(key_list[0], (NSRC, V), 1.0, 6.0, ((0, 32),))
    fetch_blocks = draw_fetch_blocks(jax.random.fold_in(key_list[11], 71), 0)
    pixel_cells = draw_pixel_cells(jax.random.fold_in(key_list[11], 71), 0)
    pixel_weights = jnp.clip(0.1 + 0.4 * jax.random.uniform(key_list[3], (KP, ROWS, TC), jnp.float32) ** shard_levels(key_list[3], (KP, ROWS, TC), ((1, 32),), -0.2, 0.2), 0.1, 0.5)
    seam_flip = draw_seam_flip(jax.random.fold_in(key_list[11], 71), 0)
    encode_weight = centred(key_list[5], (V, CH), V ** -0.5, 0.5)
    encode_bias = centred(key_list[6], (CH,), 0.5, 3.0, (), jnp.float32)
    first_kernel = centred(key_list[7], (3, 3, CH, CH), (9 * CH) ** -0.5, 0.25)
    first_bias = centred(key_list[8], (CH,), 0.5, 3.0, (), jnp.float32)
    second_kernel = centred(key_list[9], (3, 3, CH, CH), (9 * CH) ** -0.5, 0.25)
    second_bias = centred(key_list[10], (CH,), 0.5, 3.0, (), jnp.float32)
    return dict(source=source, fetch_blocks=fetch_blocks, pixel_cells=pixel_cells, pixel_weights=pixel_weights, seam_flip=seam_flip, encode_weight=encode_weight, encode_bias=encode_bias, first_kernel=first_kernel, first_bias=first_bias, second_kernel=second_kernel, second_bias=second_bias)


def regrid_encode(source, fetch_blocks, pixel_cells, pixel_weights, encode_weight, encode_bias):
    pixel_count = SR * TC

    def one_device(packed):
        device, cell_ids, weights = packed
        device_plan = lax.dynamic_index_in_dim(fetch_blocks, device, 1, keepdims=False)
        slot_number = cell_ids // (DEVICES * SB)
        owner_device = (cell_ids // SB) % DEVICES
        within = cell_ids % SB
        chosen = device_plan[slot_number, owner_device]
        source_row = owner_device * (SBLK * SB) + jnp.maximum(chosen, 0) * SB + within
        values = jnp.take(source, source_row.reshape(-1), axis=0).reshape(KP, pixel_count, V).astype(jnp.float32)
        values = jnp.where((chosen >= 0)[..., None], values, jnp.zeros((), jnp.float32))
        regridded = jnp.sum(weights[..., None] * values, axis=0).astype(jnp.bfloat16)
        projected = jnp.dot(regridded, encode_weight, preferred_element_type=jnp.float32) + encode_bias
        return projected.astype(jnp.bfloat16)

    devices = jnp.arange(DEVICES, dtype=jnp.int32)
    cell_ids = jnp.transpose(pixel_cells.reshape(KP, DEVICES, pixel_count), (1, 0, 2))
    weights = jnp.transpose(pixel_weights.reshape(KP, DEVICES, pixel_count), (1, 0, 2))
    encoded = lax.map(one_device, (devices, cell_ids, weights))
    return jnp.transpose(encoded.reshape(DEVICES * SR, TC, CH), (2, 0, 1))


def pad_image(feature_map, seam_flip):
    tile_grid = feature_map.reshape(CH, TILES, TILE_ROWS, TC)
    tile_grid = jnp.pad(tile_grid, ((0, 0), (0, 0), (1, 1), (0, 0)))
    leading_column = jnp.roll(tile_grid[..., -1:], 1, axis=1)
    trailing_column = jnp.roll(tile_grid[..., :1], -1, axis=1)
    flip_leading = (jnp.roll(seam_flip, 1) > 0)[None, :, None, None]
    flip_trailing = (seam_flip > 0)[None, :, None, None]
    leading_column = jnp.where(flip_leading, leading_column[:, :, ::-1, :], leading_column)
    trailing_column = jnp.where(flip_trailing, trailing_column[:, :, ::-1, :], trailing_column)
    return jnp.concatenate((leading_column, tile_grid, trailing_column), axis=3)


def conv_tile(tile_data, filters):
    result = lax.conv_general_dilated(tile_data[None].astype(jnp.float32), filters, (1, 1), "VALID", dimension_numbers=("NCHW", "OIHW", "NCHW"), precision=lax.Precision.HIGHEST)
    return result[0]


def untile(stacked):
    return jnp.transpose(stacked, (1, 0, 2, 3)).reshape(CH, TILES * TILE_ROWS, TC)


def reference(source, fetch_blocks, pixel_cells, pixel_weights, seam_flip, encode_weight, encode_bias, first_kernel, first_bias, second_kernel, second_bias):
    encoded = regrid_encode(source, fetch_blocks, pixel_cells, pixel_weights, encode_weight, encode_bias)
    first_filters = jnp.transpose(first_kernel.astype(jnp.float32), (2, 3, 0, 1))
    second_filters = jnp.transpose(second_kernel.astype(jnp.float32), (2, 3, 0, 1))

    def first_layer(tile_data):
        summed = conv_tile(tile_data, first_filters) + first_bias[:, None, None]
        return jax.nn.silu(summed).astype(jnp.bfloat16)

    hidden = untile(lax.map(first_layer, jnp.moveaxis(pad_image(encoded, seam_flip), 1, 0)))

    def second_layer(packed):
        tile_data, residual = packed
        summed = conv_tile(tile_data, second_filters) + second_bias[:, None, None]
        return (summed + residual.astype(jnp.float32)).astype(jnp.bfloat16)

    residual_tiles = jnp.moveaxis(encoded.reshape(CH, TILES, TILE_ROWS, TC), 1, 0)
    features = lax.map(second_layer, (jnp.moveaxis(pad_image(hidden, seam_flip), 1, 0), residual_tiles))
    return untile(features)
```

```python
import functools

import jax
import jax.numpy as jnp
from jax import lax
from jax.experimental import pallas as pl
from jax.experimental.pallas import tpu as pltpu
from jax.sharding import PartitionSpec as P

SB = 64
LANES = 128
VMEM_LIMIT = 48 * 1024 * 1024


def vmem():
    return pl.BlockSpec(memory_space=pltpu.VMEM)


def smem():
    return pl.BlockSpec(memory_space=pltpu.SMEM)


def params():
    return pltpu.CompilerParams(vmem_limit_bytes=VMEM_LIMIT)


def project_kernel(wanted_ref, source_ref, weight_ref, out_ref, stored):
    tiles = source_ref.shape[0] // LANES
    half = weight_ref.shape[1] // 2
    low_lanes = lax.broadcasted_iota(jnp.int32, (half, LANES), 1) < SB

    def one_tile(t, carry):
        cells = source_ref[pl.ds(pl.multiple_of(t * LANES, LANES), LANES), :]
        x = lax.dot_general(
            weight_ref[...], cells, (((0,), (1,)), ((), ())), preferred_element_type=jnp.float32
        )
        top, bottom = x[:half], x[half:]
        stored[2 * t] = jnp.where(low_lanes, top, pltpu.roll(bottom, SB, 1)).astype(jnp.bfloat16)
        stored[2 * t + 1] = jnp.where(low_lanes, pltpu.roll(top, SB, 1), bottom).astype(
            jnp.bfloat16
        )
        return carry

    lax.fori_loop(0, tiles, one_tile, 0, unroll=4)

    def one_request(n, carry):
        w = wanted_ref[n]
        block = stored[jnp.maximum(w, 0)]
        out_ref[n] = jnp.where(w >= 0, block, jnp.zeros_like(block))
        return carry

    lax.fori_loop(0, out_ref.shape[0], one_request, 0, unroll=4)


def project_blocks(source, wanted, encode_weight):
    count = wanted.shape[0]
    blocks = source.shape[0] // SB
    half = encode_weight.shape[1] // 2
    return pl.pallas_call(
        project_kernel,
        out_shape=jax.ShapeDtypeStruct((count, half, LANES), jnp.bfloat16),
        in_specs=[smem(), vmem(), vmem()],
        out_specs=vmem(),
        scratch_shapes=[pltpu.VMEM((blocks, half, LANES), jnp.bfloat16)],
        compiler_params=params(),
    )(wanted, source, encode_weight)


def edge_insert(edge_ref, side, r, column):
    lane = lax.broadcasted_iota(jnp.int32, edge_ref.shape[1:], 1)
    edge_ref[side] = jnp.where(lane == r, column, edge_ref[side])


def spread(ref, k, r, first):
    base = pl.multiple_of(r // 8 * 8, 8)
    block = ref[k, pl.ds(base, 8), first : first + LANES]
    pick = jnp.full((8, LANES), r - base, jnp.int32)
    return jnp.take_along_axis(block, pick, axis=0, mode="promise_in_bounds")


def lookup_kernel(blocks_ref, cells_ref, weights_ref, bias_ref, out_ref, edge_ref, table, scales):
    terms, rows, cols = cells_ref.shape
    tiles, half = table.shape[0], table.shape[1]
    groups = half // 8
    low_lanes = lax.broadcasted_iota(jnp.int32, (half, LANES), 1) < SB

    def halves(t):
        first = blocks_ref[2 * t].astype(jnp.float32)
        second = blocks_ref[2 * t + 1].astype(jnp.float32)
        top = jnp.where(low_lanes, first, pltpu.roll(second, SB, 1))
        bottom = jnp.where(low_lanes, pltpu.roll(first, SB, 1), second)
        return top, bottom

    def largest(t, carry):
        top, bottom = halves(t)
        return jnp.maximum(carry[0], jnp.abs(top)), jnp.maximum(carry[1], jnp.abs(bottom))

    zero = jnp.zeros((half, LANES), jnp.float32)
    found = lax.fori_loop(0, tiles, largest, (zero, zero), unroll=4)
    tops = [jnp.maximum(jnp.max(m, axis=1, keepdims=True), 1e-30) for m in found]
    up = [jnp.broadcast_to(32000.0 / m, (half, LANES)) for m in tops]
    scales[0] = jnp.broadcast_to(tops[0] * (1.0 / 32000.0), (half, LANES))
    scales[1] = jnp.broadcast_to(tops[1] * (1.0 / 32000.0), (half, LANES))

    def pack(t, carry):
        top, bottom = halves(t)
        high = jnp.round(top * up[0]).astype(jnp.int32)
        low = jnp.round(bottom * up[1]).astype(jnp.int32)
        table[t] = (high << 16) | (low & 0xFFFF)
        return carry

    lax.fori_loop(0, tiles, pack, 0, unroll=2)
    edge_ref[...] = jnp.zeros_like(edge_ref)

    def one_row(r, carry):
        pieces = []
        for first in range(0, cols, LANES):
            index, tile, weight = [], [], []
            for k in range(terms):
                cell = spread(cells_ref, k, r, first)
                index.append(cell & (LANES - 1))
                tile.append(cell >> 7)
                weight.append(spread(weights_ref, k, r, first))
            got = [[jnp.zeros((8, LANES), jnp.int32)] * groups for _ in range(terms)]

            def some_tiles(t0, got):
                got = [list(g) for g in got]
                for dt in range(min(tiles, 32)):
                    t = t0 * min(tiles, 32) + dt
                    entries = [table[t, 8 * g : 8 * g + 8, :] for g in range(groups)]
                    for k in range(terms):
                        here = tile[k] == t
                        for g in range(groups):
                            value = jnp.take_along_axis(
                                entries[g], index[k], axis=1, mode="promise_in_bounds"
                            )
                            got[k][g] = jnp.where(here, value, got[k][g])
                return got

            if tiles <= 32:
                got = some_tiles(0, got)
            else:
                got = lax.fori_loop(0, tiles // 32, some_tiles, got)
            parts = [[], []]
            for g in range(groups):
                high = jnp.zeros((8, LANES), jnp.float32)
                low = jnp.zeros((8, LANES), jnp.float32)
                for k in range(terms):
                    high += (got[k][g] >> 16).astype(jnp.float32) * weight[k]
                    low += ((got[k][g] << 16) >> 16).astype(jnp.float32) * weight[k]
                parts[0].append(high * scales[0, 8 * g : 8 * g + 8, :])
                parts[1].append(low * scales[1, 8 * g : 8 * g + 8, :])
            pieces.append(jnp.concatenate(parts[0] + parts[1], axis=0) + bias_ref[...])
        value = jnp.concatenate(pieces, axis=1).astype(jnp.bfloat16)
        out_ref[r] = value
        edge_insert(edge_ref, 0, r, pieces[0][:, :1])
        edge_insert(edge_ref, 1, r, pieces[-1][:, LANES - 1 :])
        return carry

    lax.fori_loop(0, rows, one_row, 0)


def lookup(blocks, pixel_cells, pixel_weights, encode_bias):
    terms, rows, cols = pixel_cells.shape
    count, half, lanes = blocks.shape
    channels = 2 * half
    return pl.pallas_call(
        lookup_kernel,
        out_shape=(
            jax.ShapeDtypeStruct((rows, channels, cols), jnp.bfloat16),
            jax.ShapeDtypeStruct((2, channels, LANES), jnp.float32),
        ),
        in_specs=[vmem()] * 4,
        out_specs=(vmem(), vmem()),
        scratch_shapes=[
            pltpu.VMEM((count // 2, half, LANES), jnp.int32),
            pltpu.VMEM((2, half, LANES), jnp.float32),
        ],
        compiler_params=params(),
    )(blocks, pixel_cells, pixel_weights, encode_bias[:, None])


def conv_kernel(last, x_ref, top_ref, bottom_ref, side_ref, matrix_ref, bias_ref, *rest):
    if last:
        residual_ref, out_ref, stack = rest
    else:
        out_ref, edge_ref, stack = rest
        edge_ref[...] = jnp.zeros_like(edge_ref)
    rows, channels, cols = x_ref.shape
    lane = lax.broadcasted_iota(jnp.int32, (channels, cols), 1)
    side_lane = lax.broadcasted_iota(jnp.int32, (channels, LANES), 1)

    def build(p, row):
        wide = row.astype(jnp.float32)
        picked = [
            jnp.sum(jnp.where(side_lane == p, side_ref[s], 0.0), axis=1, keepdims=True)
            for s in range(2)
        ]
        left = jnp.where(lane == 0, picked[0], pltpu.roll(wide, 1, 1))
        right = jnp.where(lane == cols - 1, picked[1], pltpu.roll(wide, cols - 1, 1))
        stack[p, :channels] = left.astype(jnp.bfloat16)
        stack[p, channels : 2 * channels] = row
        stack[p, 2 * channels :] = right.astype(jnp.bfloat16)

    build(0, top_ref[...])
    build(rows + 1, bottom_ref[...])

    def fill(r, carry):
        build(r + 1, x_ref[r])
        return carry

    lax.fori_loop(0, rows, fill, 0, unroll=4)

    def one_row(r, carry):
        window = stack[pl.ds(r, 3)].reshape(9 * channels, cols)
        summed = (
            jnp.dot(matrix_ref[...], window, preferred_element_type=jnp.float32) + bias_ref[...]
        )
        if last:
            out_ref[r] = (summed + residual_ref[r].astype(jnp.float32)).astype(jnp.bfloat16)
        else:
            hidden = summed / (1.0 + jnp.exp(-summed))
            out_ref[r] = hidden.astype(jnp.bfloat16)
            edge_insert(edge_ref, 0, r, hidden[:, :1])
            edge_insert(edge_ref, 1, r, hidden[:, cols - 1 :])
        return carry

    lax.fori_loop(0, rows, one_row, 0, unroll=4)


def conv(x, halo, matrix, bias, residual=None):
    rows, channels, cols = x.shape
    last = residual is not None
    grid_shape = jax.ShapeDtypeStruct(x.shape, jnp.bfloat16)
    edge_shape = jax.ShapeDtypeStruct((2, channels, LANES), jnp.float32)
    operands = (x,) + halo + (matrix, bias[:, None]) + ((residual,) if last else ())
    return pl.pallas_call(
        functools.partial(conv_kernel, last),
        out_shape=grid_shape if last else (grid_shape, edge_shape),
        in_specs=[vmem()] * len(operands),
        out_specs=vmem() if last else (vmem(), vmem()),
        scratch_shapes=[pltpu.VMEM((rows + 2, 3 * channels, cols), jnp.bfloat16)],
        compiler_params=params(),
    )(*operands)


def halos(x, edges, seam_flip):
    rows = x.shape[0]
    subs, tiles = lax.axis_size("sub"), lax.axis_size("tile")
    sub, tile = lax.axis_index("sub"), lax.axis_index("tile")
    down = [(i, i + 1) for i in range(subs - 1)]
    up = [(i + 1, i) for i in range(subs - 1)]
    right = [(i, (i + 1) % tiles) for i in range(tiles)]
    left = [((i + 1) % tiles, i) for i in range(tiles)]
    top = lax.ppermute(x[rows - 1], "sub", down)
    bottom = lax.ppermute(x[0], "sub", up)
    edges = edges.astype(jnp.bfloat16)
    beside = jnp.stack(
        (lax.ppermute(edges[1], "tile", right), lax.ppermute(edges[0], "tile", left))
    )
    gathered = lax.all_gather(beside, "sub")[..., :rows]
    whole = jnp.moveaxis(gathered, 0, 2).reshape(2, x.shape[1], subs * rows)
    whole = jnp.pad(whole, ((0, 0), (0, 0), (1, 1)))
    flips = jnp.stack((seam_flip[(tile + tiles - 1) % tiles], seam_flip[tile]))
    whole = jnp.where(flips[:, None, None] > 0, whole[..., ::-1], whole)
    sides = lax.dynamic_slice_in_dim(whole, sub * rows, rows + 2, 2).astype(jnp.float32)
    sides = jnp.pad(sides, ((0, 0), (0, 0), (0, LANES - rows - 2)))
    return top, bottom, sides


def kernel_matrix(kernel):
    return jnp.transpose(kernel, (2, 0, 1, 3)).reshape(kernel.shape[2], -1)


def shards(
    source,
    fetch_blocks,
    pixel_cells,
    pixel_weights,
    seam_flip,
    encode_weight,
    encode_bias,
    first_kernel,
    first_bias,
    second_kernel,
    second_bias,
):
    wanted = lax.all_to_all(fetch_blocks, ("tile", "sub"), split_axis=2, concat_axis=1, tiled=True)
    slots, devices = wanted.shape[0], wanted.shape[1]
    chosen = project_blocks(source, wanted.reshape(-1), encode_weight)
    chosen = chosen.reshape((slots, devices) + chosen.shape[1:])
    arrived = lax.all_to_all(chosen, ("tile", "sub"), split_axis=1, concat_axis=1, tiled=True)
    blocks = arrived.reshape((-1,) + arrived.shape[2:])
    encoded, edges = lookup(blocks, pixel_cells, pixel_weights, encode_bias)
    hidden, hidden_edges = conv(
        encoded, halos(encoded, edges, seam_flip), kernel_matrix(first_kernel), first_bias
    )
    features = conv(
        hidden,
        halos(hidden, hidden_edges, seam_flip),
        kernel_matrix(second_kernel),
        second_bias,
        encoded,
    )
    return jnp.transpose(features, (1, 0, 2))


def solution(mesh):
    in_specs = (
        P(("tile", "sub"), None),
        P(None, ("tile", "sub"), None),
        P(None, ("tile", "sub"), None),
        P(None, ("tile", "sub"), None),
        P(),
        P(),
        P(),
        P(),
        P(),
        P(),
        P(),
    )
    out_specs = P(None, ("tile", "sub"), None)
    return jax.shard_map(shards, mesh=mesh, in_specs=in_specs, out_specs=out_specs, check_vma=False)
```

```python
import functools

import jax
import jax.numpy as jnp
from jax import lax
from jax.experimental import pallas as pl
from jax.experimental.pallas import tpu as pltpu
from jax.sharding import PartitionSpec as P

SB = 64
LANES = 128
VMEM_LIMIT = 48 * 1024 * 1024


def vmem():
    return pl.BlockSpec(memory_space=pltpu.VMEM)


def smem():
    return pl.BlockSpec(memory_space=pltpu.SMEM)


def params():
    return pltpu.CompilerParams(vmem_limit_bytes=VMEM_LIMIT)


def project_kernel(wanted_ref, source_ref, weight_ref, out_ref, stored):
    tiles = source_ref.shape[0] // LANES
    half = weight_ref.shape[1] // 2
    low_lanes = lax.broadcasted_iota(jnp.int32, (half, LANES), 1) < SB

    def one_tile(t, carry):
        cells = source_ref[pl.ds(pl.multiple_of(t * LANES, LANES), LANES), :]
        x = lax.dot_general(
            weight_ref[...], cells, (((0,), (1,)), ((), ())), preferred_element_type=jnp.float32
        )
        top, bottom = x[:half], x[half:]
        stored[2 * t] = jnp.where(low_lanes, top, pltpu.roll(bottom, SB, 1)).astype(jnp.bfloat16)
        stored[2 * t + 1] = jnp.where(low_lanes, pltpu.roll(top, SB, 1), bottom).astype(
            jnp.bfloat16
        )
        return carry

    lax.fori_loop(0, tiles, one_tile, 0, unroll=4)

    def one_request(n, carry):
        w = wanted_ref[n]
        block = stored[jnp.maximum(w, 0)]
        out_ref[n] = jnp.where(w >= 0, block, jnp.zeros_like(block))
        return carry

    lax.fori_loop(0, out_ref.shape[0], one_request, 0, unroll=4)


def project_blocks(source, wanted, encode_weight):
    count = wanted.shape[0]
    blocks = source.shape[0] // SB
    half = encode_weight.shape[1] // 2
    return pl.pallas_call(
        project_kernel,
        out_shape=jax.ShapeDtypeStruct((count, half, LANES), jnp.bfloat16),
        in_specs=[smem(), vmem(), vmem()],
        out_specs=vmem(),
        scratch_shapes=[pltpu.VMEM((blocks, half, LANES), jnp.bfloat16)],
        compiler_params=params(),
    )(wanted, source, encode_weight)


def edge_insert(edge_ref, side, r, column):
    lane = lax.broadcasted_iota(jnp.int32, edge_ref.shape[1:], 1)
    edge_ref[side] = jnp.where(lane == r + 1, column, edge_ref[side])


def spread(ref, k, r, first, height):
    base = pl.multiple_of(r // 8 * 8, 8)
    block = ref[k, pl.ds(base, 8), first : first + LANES]
    pick = jnp.full((8, LANES), r - base, jnp.int32)
    row = jnp.take_along_axis(block, pick, axis=0, mode="promise_in_bounds")
    return jnp.concatenate([row] * (height // 8), axis=0)


def lookup_kernel(blocks_ref, cells_ref, weights_ref, bias_ref, out_ref, edge_ref, table):
    terms, rows, cols = cells_ref.shape
    count, half = blocks_ref.shape[0], blocks_ref.shape[1]
    channels = 2 * half
    chunk, span = 4, 64
    low_lanes = lax.broadcasted_iota(jnp.int32, (half, LANES), 1) < SB

    def unpack(t, carry):
        first = blocks_ref[2 * t].astype(jnp.float32)
        second = blocks_ref[2 * t + 1].astype(jnp.float32)
        top = jnp.where(low_lanes, first, pltpu.roll(second, SB, 1))
        bottom = jnp.where(low_lanes, pltpu.roll(first, SB, 1), second)
        table[t] = jnp.concatenate((top, bottom), axis=0).astype(jnp.bfloat16)
        return carry

    lax.fori_loop(0, count // 2, unpack, 0, unroll=4)
    edge_ref[...] = jnp.zeros_like(edge_ref)
    within = lax.broadcasted_iota(jnp.int32, (SB, LANES), 0)
    zero = jnp.zeros((16, LANES), jnp.bfloat16)
    firsts = list(range(0, cols, LANES))

    def one_row(r, carry):
        block_of = [[None] * terms for _ in firsts]
        weighted = [[None] * terms for _ in firsts]
        for h, first in enumerate(firsts):
            for k in range(terms):
                inner = spread(cells_ref, k, r, first, SB) & (SB - 1)
                weight = spread(weights_ref, k, r, first, SB)
                block_of[h][k] = spread(cells_ref, k, r, first, 16) >> 6
                weighted[h][k] = jnp.where(inner == within, weight, 0.0).astype(jnp.bfloat16)

        def some_blocks(g, total):
            numbers = [
                [(b - g * span).astype(jnp.float32).astype(jnp.bfloat16) for b in side]
                for side in block_of
            ]
            for c in range(min(count, span) // chunk):
                halves = []
                for h in range(len(firsts)):
                    parts = []
                    for d in range(chunk):
                        number = jnp.asarray(c * chunk + d, jnp.bfloat16)
                        here = [numbers[h][k] == number for k in range(terms)]
                        for i in range(0, SB, 16):
                            found = [
                                jnp.where(here[k], weighted[h][k][i : i + 16], zero)
                                for k in range(terms)
                            ]
                            parts.append(sum(found[1:], found[0]))
                    halves.append(jnp.concatenate(parts, axis=0))
                at = (g * span + c * chunk) // 2
                lhs = jnp.concatenate([table[at + d] for d in range(chunk // 2)], axis=1)
                total = total + jnp.dot(
                    lhs, jnp.concatenate(halves, axis=1), preferred_element_type=jnp.float32
                )
            return total

        total = jnp.zeros((channels, cols), jnp.float32)
        if count <= span:
            total = some_blocks(0, total)
        else:
            total = lax.fori_loop(0, count // span, some_blocks, total)
        total = total + bias_ref[...]
        out_ref[r] = total.astype(jnp.bfloat16)
        edge_insert(edge_ref, 0, r, total[:, :1])
        edge_insert(edge_ref, 1, r, total[:, cols - 1 :])
        return carry

    lax.fori_loop(0, rows, one_row, 0)


def lookup(blocks, pixel_cells, pixel_weights, encode_bias):
    terms, rows, cols = pixel_cells.shape
    count, half, lanes = blocks.shape
    channels = 2 * half
    return pl.pallas_call(
        lookup_kernel,
        out_shape=(
            jax.ShapeDtypeStruct((rows, channels, cols), jnp.bfloat16),
            jax.ShapeDtypeStruct((2, channels, LANES), jnp.float32),
        ),
        in_specs=[vmem()] * 4,
        out_specs=(vmem(), vmem()),
        scratch_shapes=[pltpu.VMEM((count // 2, channels, LANES), jnp.bfloat16)],
        compiler_params=params(),
    )(blocks, pixel_cells, pixel_weights, encode_bias[:, None])


def conv_kernel(last, x_ref, top_ref, bottom_ref, side_ref, matrix_ref, bias_ref, *rest):
    if last:
        residual_ref, out_ref, taps = rest
    else:
        out_ref, edge_ref, taps = rest
        edge_ref[...] = jnp.zeros_like(edge_ref)
    rows, channels, cols = x_ref.shape
    lane = lax.broadcasted_iota(jnp.int32, (channels, cols), 1)
    side_lane = lax.broadcasted_iota(jnp.int32, (channels, LANES), 1)

    def multiply(p, row):
        wide = row.astype(jnp.float32)
        picked = [
            jnp.sum(jnp.where(side_lane == p, side_ref[s], 0.0), axis=1, keepdims=True)
            for s in range(2)
        ]
        left = jnp.where(lane == 0, picked[0], pltpu.roll(wide, 1, 1))
        right = jnp.where(lane == cols - 1, picked[1], pltpu.roll(wide, cols - 1, 1))
        beside = jnp.concatenate(
            (left.astype(jnp.bfloat16), row, right.astype(jnp.bfloat16)), axis=0
        )
        taps[p] = jnp.dot(matrix_ref[...], beside, preferred_element_type=jnp.float32)

    multiply(0, top_ref[...])
    multiply(rows + 1, bottom_ref[...])

    def fill(r, carry):
        multiply(r + 1, x_ref[r])
        return carry

    lax.fori_loop(0, rows, fill, 0, unroll=4)

    def one_row(r, carry):
        summed = bias_ref[...] + (
            taps[r, :channels]
            + taps[r + 1, channels : 2 * channels]
            + taps[r + 2, 2 * channels :]
        )
        if last:
            out_ref[r] = (summed + residual_ref[r].astype(jnp.float32)).astype(jnp.bfloat16)
        else:
            hidden = summed / (1.0 + jnp.exp(-summed))
            out_ref[r] = hidden.astype(jnp.bfloat16)
            edge_insert(edge_ref, 0, r, hidden[:, :1])
            edge_insert(edge_ref, 1, r, hidden[:, cols - 1 :])
        return carry

    lax.fori_loop(0, rows, one_row, 0, unroll=4)


def conv(x, halo, matrix, bias, residual=None):
    rows, channels, cols = x.shape
    last = residual is not None
    grid_shape = jax.ShapeDtypeStruct(x.shape, jnp.bfloat16)
    edge_shape = jax.ShapeDtypeStruct((2, channels, LANES), jnp.float32)
    operands = (x,) + halo + (matrix, bias[:, None]) + ((residual,) if last else ())
    return pl.pallas_call(
        functools.partial(conv_kernel, last),
        out_shape=grid_shape if last else (grid_shape, edge_shape),
        in_specs=[vmem()] * len(operands),
        out_specs=vmem() if last else (vmem(), vmem()),
        scratch_shapes=[pltpu.VMEM((rows + 2, 3 * channels, cols), jnp.float32)],
        compiler_params=params(),
    )(*operands)


def halos(x, edges, seam_flip):
    rows, channels, cols = x.shape
    subs, tiles = lax.axis_size("sub"), lax.axis_size("tile")
    tile = lax.axis_index("tile")
    down = [(i, i + 1) for i in range(subs - 1)]
    up = [(i + 1, i) for i in range(subs - 1)]
    top = lax.ppermute(x[rows - 1], "sub", down)
    bottom = lax.ppermute(x[0], "sub", up)
    lane = lax.broadcasted_iota(jnp.int32, (channels, LANES), 1)

    def side(s, step):
        c = (cols - 1) * s
        edge = edges[s].astype(jnp.bfloat16)
        edge = jnp.where(lane == 0, top[:, c : c + 1], edge)
        edge = jnp.where(lane == rows + 1, bottom[:, c : c + 1], edge)
        straight = [
            (t * subs + q, (t + step) % tiles * subs + q)
            for t in range(tiles)
            for q in range(subs)
        ]
        mirrored = [
            (t * subs + q, (t + step) % tiles * subs + subs - 1 - q)
            for t in range(tiles)
            for q in range(subs)
        ]
        return (
            lax.ppermute(edge, ("tile", "sub"), straight),
            lax.ppermute(edge, ("tile", "sub"), mirrored),
        )

    from_left, from_right = side(1, 1), side(0, -1)
    flips = (seam_flip[(tile + tiles - 1) % tiles], seam_flip[tile])
    chosen = []
    for (straight, mirrored), flip in zip((from_left, from_right), flips):
        turned = mirrored[:, : rows + 2][:, ::-1]
        turned = jnp.pad(turned, ((0, 0), (0, LANES - rows - 2)))
        chosen.append(jnp.where(flip > 0, turned, straight).astype(jnp.float32))
    return top, bottom, jnp.stack(chosen)


def kernel_matrix(kernel):
    size = kernel.shape[0] * kernel.shape[2]
    return jnp.transpose(kernel, (0, 2, 1, 3)).reshape(size, -1)


def shards(
    source,
    fetch_blocks,
    pixel_cells,
    pixel_weights,
    seam_flip,
    encode_weight,
    encode_bias,
    first_kernel,
    first_bias,
    second_kernel,
    second_bias,
):
    wanted = lax.all_to_all(fetch_blocks, ("tile", "sub"), split_axis=2, concat_axis=1, tiled=True)
    slots, devices = wanted.shape[0], wanted.shape[1]
    chosen = project_blocks(source, wanted.reshape(-1), encode_weight)
    chosen = chosen.reshape((slots, devices) + chosen.shape[1:])
    arrived = lax.all_to_all(chosen, ("tile", "sub"), split_axis=1, concat_axis=1, tiled=True)
    blocks = arrived.reshape((-1,) + arrived.shape[2:])
    encoded, edges = lookup(blocks, pixel_cells, pixel_weights, encode_bias)
    hidden, hidden_edges = conv(
        encoded, halos(encoded, edges, seam_flip), kernel_matrix(first_kernel), first_bias
    )
    features = conv(
        hidden,
        halos(hidden, hidden_edges, seam_flip),
        kernel_matrix(second_kernel),
        second_bias,
        encoded,
    )
    return jnp.transpose(features, (1, 0, 2))


def solution(mesh):
    in_specs = (
        P(("tile", "sub"), None),
        P(None, ("tile", "sub"), None),
        P(None, ("tile", "sub"), None),
        P(None, ("tile", "sub"), None),
        P(),
        P(),
        P(),
        P(),
        P(),
        P(),
        P(),
    )
    out_specs = P(None, ("tile", "sub"), None)
    return jax.shard_map(shards, mesh=mesh, in_specs=in_specs, out_specs=out_specs, check_vma=False)
```

```python
import functools

import jax
import jax.numpy as jnp
from jax import lax
from jax.experimental import pallas as pl
from jax.experimental.pallas import tpu as pltpu
from jax.sharding import PartitionSpec as P

SB = 64
LANES = 128
VMEM_LIMIT = 48 * 1024 * 1024


def vmem():
    return pl.BlockSpec(memory_space=pltpu.VMEM)


def smem():
    return pl.BlockSpec(memory_space=pltpu.SMEM)


def params():
    return pltpu.CompilerParams(vmem_limit_bytes=VMEM_LIMIT)


def project_kernel(wanted_ref, source_ref, weight_ref, out_ref, stored):
    tiles = source_ref.shape[0] // LANES
    half = weight_ref.shape[1] // 2
    low_lanes = lax.broadcasted_iota(jnp.int32, (half, LANES), 1) < SB

    def one_tile(t, carry):
        cells = source_ref[pl.ds(pl.multiple_of(t * LANES, LANES), LANES), :]
        x = lax.dot_general(
            weight_ref[...], cells, (((0,), (1,)), ((), ())), preferred_element_type=jnp.float32
        )
        top, bottom = x[:half], x[half:]
        stored[2 * t] = jnp.where(low_lanes, top, pltpu.roll(bottom, SB, 1)).astype(jnp.bfloat16)
        stored[2 * t + 1] = jnp.where(low_lanes, pltpu.roll(top, SB, 1), bottom).astype(
            jnp.bfloat16
        )
        return carry

    lax.fori_loop(0, tiles, one_tile, 0, unroll=4)

    def one_request(n, carry):
        w = wanted_ref[n]
        block = stored[jnp.maximum(w, 0)]
        out_ref[n] = jnp.where(w >= 0, block, jnp.zeros_like(block))
        return carry

    lax.fori_loop(0, out_ref.shape[0], one_request, 0, unroll=4)


def project_blocks(source, wanted, encode_weight):
    count = wanted.shape[0]
    blocks = source.shape[0] // SB
    half = encode_weight.shape[1] // 2
    return pl.pallas_call(
        project_kernel,
        out_shape=jax.ShapeDtypeStruct((count, half, LANES), jnp.bfloat16),
        in_specs=[smem(), vmem(), vmem()],
        out_specs=vmem(),
        scratch_shapes=[pltpu.VMEM((blocks, half, LANES), jnp.bfloat16)],
        compiler_params=params(),
    )(wanted, source, encode_weight)


def edge_insert(edge_ref, side, r, column):
    lane = lax.broadcasted_iota(jnp.int32, edge_ref.shape[1:], 1)
    edge_ref[side] = jnp.where(lane == r + 1, column, edge_ref[side])


def spread(ref, k, r, first, height):
    base = pl.multiple_of(r // 8 * 8, 8)
    block = ref[k, pl.ds(base, 8), first : first + LANES]
    pick = jnp.full((8, LANES), r - base, jnp.int32)
    row = jnp.take_along_axis(block, pick, axis=0, mode="promise_in_bounds")
    return jnp.concatenate([row] * (height // 8), axis=0)


def lookup_kernel(blocks_ref, cells_ref, weights_ref, bias_ref, out_ref, edge_ref, table):
    terms, rows, cols = cells_ref.shape
    count, half = blocks_ref.shape[0], blocks_ref.shape[1]
    channels = 2 * half
    chunk, span = 4, 64
    low_lanes = lax.broadcasted_iota(jnp.int32, (half, LANES), 1) < SB

    def unpack(t, carry):
        first = blocks_ref[2 * t].astype(jnp.float32)
        second = blocks_ref[2 * t + 1].astype(jnp.float32)
        top = jnp.where(low_lanes, first, pltpu.roll(second, SB, 1))
        bottom = jnp.where(low_lanes, pltpu.roll(first, SB, 1), second)
        table[t] = jnp.concatenate((top, bottom), axis=0).astype(jnp.bfloat16)
        return carry

    lax.fori_loop(0, count // 2, unpack, 0, unroll=4)
    edge_ref[...] = jnp.zeros_like(edge_ref)
    within = lax.broadcasted_iota(jnp.int32, (SB, LANES), 0)
    zero = jnp.zeros((16, LANES), jnp.bfloat16)
    firsts = list(range(0, cols, LANES))

    def one_row(r, carry):
        block_of = [[None] * terms for _ in firsts]
        weighted = [[None] * terms for _ in firsts]
        for h, first in enumerate(firsts):
            for k in range(terms):
                inner = spread(cells_ref, k, r, first, SB) & (SB - 1)
                weight = spread(weights_ref, k, r, first, SB)
                block_of[h][k] = spread(cells_ref, k, r, first, 16) >> 6
                weighted[h][k] = jnp.where(inner == within, weight, 0.0).astype(jnp.bfloat16)

        def some_blocks(g, total):
            numbers = [
                [(b - g * span).astype(jnp.float32).astype(jnp.bfloat16) for b in side]
                for side in block_of
            ]
            for c in range(min(count, span) // chunk):
                halves = []
                for h in range(len(firsts)):
                    parts = []
                    for d in range(chunk):
                        number = jnp.asarray(c * chunk + d, jnp.bfloat16)
                        here = [numbers[h][k] == number for k in range(terms)]
                        for i in range(0, SB, 16):
                            found = [
                                jnp.where(here[k], weighted[h][k][i : i + 16], zero)
                                for k in range(terms)
                            ]
                            parts.append(sum(found[1:], found[0]))
                    halves.append(jnp.concatenate(parts, axis=0))
                at = (g * span + c * chunk) // 2
                lhs = jnp.concatenate([table[at + d] for d in range(chunk // 2)], axis=1)
                total = total + jnp.dot(
                    lhs, jnp.concatenate(halves, axis=1), preferred_element_type=jnp.float32
                )
            return total

        total = jnp.zeros((channels, cols), jnp.float32)
        if count <= span:
            total = some_blocks(0, total)
        else:
            total = lax.fori_loop(0, count // span, some_blocks, total)
        total = total + bias_ref[...]
        out_ref[r] = total.astype(jnp.bfloat16)
        edge_insert(edge_ref, 0, r, total[:, :1])
        edge_insert(edge_ref, 1, r, total[:, cols - 1 :])
        return carry

    lax.fori_loop(0, rows, one_row, 0)


def lookup(blocks, pixel_cells, pixel_weights, encode_bias):
    terms, rows, cols = pixel_cells.shape
    count, half, lanes = blocks.shape
    channels = 2 * half
    return pl.pallas_call(
        lookup_kernel,
        out_shape=(
            jax.ShapeDtypeStruct((rows, channels, cols), jnp.bfloat16),
            jax.ShapeDtypeStruct((2, channels, LANES), jnp.float32),
        ),
        in_specs=[vmem()] * 4,
        out_specs=(vmem(), vmem()),
        scratch_shapes=[pltpu.VMEM((count // 2, channels, LANES), jnp.bfloat16)],
        compiler_params=params(),
    )(blocks, pixel_cells, pixel_weights, encode_bias[:, None])


def conv_kernel(last, x_ref, top_ref, bottom_ref, side_ref, matrix_ref, bias_ref, *rest):
    if last:
        residual_ref, out_ref, stack = rest
    else:
        out_ref, edge_ref, stack = rest
        edge_ref[...] = jnp.zeros_like(edge_ref)
    rows, channels, cols = x_ref.shape
    lane = lax.broadcasted_iota(jnp.int32, (channels, cols), 1)
    side_lane = lax.broadcasted_iota(jnp.int32, (channels, LANES), 1)

    def place(p, row):
        wide = row.astype(jnp.float32)
        at = jnp.full((channels, LANES), p, jnp.int32)
        picked = [
            jnp.concatenate(
                [jnp.take_along_axis(side_ref[s], at, axis=1, mode="promise_in_bounds")]
                * (cols // LANES),
                axis=1,
            )
            for s in range(2)
        ]
        left = jnp.where(lane == 0, picked[0], pltpu.roll(wide, 1, 1))
        right = jnp.where(lane == cols - 1, picked[1], pltpu.roll(wide, cols - 1, 1))
        beside = jnp.concatenate(
            (left.astype(jnp.bfloat16), row, right.astype(jnp.bfloat16)), axis=0
        )
        stack[p] = beside

    place(0, top_ref[...])
    place(rows + 1, bottom_ref[...])

    def fill(r, carry):
        place(r + 1, x_ref[r])
        return carry

    lax.fori_loop(0, rows, fill, 0, unroll=16)

    def one_row(r, carry):
        window = stack[pl.ds(r, 3)].reshape(9 * channels, cols)
        summed = bias_ref[...] + jnp.dot(
            matrix_ref[...], window, preferred_element_type=jnp.float32
        )
        if last:
            out_ref[r] = (summed + residual_ref[r].astype(jnp.float32)).astype(jnp.bfloat16)
        else:
            hidden = summed / (1.0 + jnp.exp(-summed))
            out_ref[r] = hidden.astype(jnp.bfloat16)
            edge_insert(edge_ref, 0, r, hidden[:, :1])
            edge_insert(edge_ref, 1, r, hidden[:, cols - 1 :])
        return carry

    lax.fori_loop(0, rows, one_row, 0, unroll=16)


def conv(x, halo, matrix, bias, residual=None):
    rows, channels, cols = x.shape
    last = residual is not None
    grid_shape = jax.ShapeDtypeStruct(x.shape, jnp.bfloat16)
    edge_shape = jax.ShapeDtypeStruct((2, channels, LANES), jnp.float32)
    operands = (x,) + halo + (matrix, bias[:, None]) + ((residual,) if last else ())
    return pl.pallas_call(
        functools.partial(conv_kernel, last),
        out_shape=grid_shape if last else (grid_shape, edge_shape),
        in_specs=[vmem()] * len(operands),
        out_specs=vmem() if last else (vmem(), vmem()),
        scratch_shapes=[pltpu.VMEM((rows + 2, 3 * channels, cols), jnp.bfloat16)],
        compiler_params=params(),
    )(*operands)


def halos(x, edges, seam_flip):
    rows, channels, cols = x.shape
    subs, tiles = lax.axis_size("sub"), lax.axis_size("tile")
    tile = lax.axis_index("tile")
    down = [(i, i + 1) for i in range(subs - 1)]
    up = [(i + 1, i) for i in range(subs - 1)]
    top = lax.ppermute(x[rows - 1], "sub", down)
    bottom = lax.ppermute(x[0], "sub", up)
    lane = lax.broadcasted_iota(jnp.int32, (channels, LANES), 1)

    def side(s, step):
        c = (cols - 1) * s
        edge = edges[s].astype(jnp.bfloat16)
        edge = jnp.where(lane == 0, top[:, c : c + 1], edge)
        edge = jnp.where(lane == rows + 1, bottom[:, c : c + 1], edge)
        straight = [
            (t * subs + q, (t + step) % tiles * subs + q)
            for t in range(tiles)
            for q in range(subs)
        ]
        mirrored = [
            (t * subs + q, (t + step) % tiles * subs + subs - 1 - q)
            for t in range(tiles)
            for q in range(subs)
        ]
        return (
            lax.ppermute(edge, ("tile", "sub"), straight),
            lax.ppermute(edge, ("tile", "sub"), mirrored),
        )

    from_left, from_right = side(1, 1), side(0, -1)
    flips = (seam_flip[(tile + tiles - 1) % tiles], seam_flip[tile])
    chosen = []
    for (straight, mirrored), flip in zip((from_left, from_right), flips):
        turned = mirrored[:, : rows + 2][:, ::-1]
        turned = jnp.pad(turned, ((0, 0), (0, LANES - rows - 2)))
        chosen.append(jnp.where(flip > 0, turned, straight).astype(jnp.float32))
    return top, bottom, jnp.stack(chosen)


def kernel_matrix(kernel):
    return jnp.transpose(kernel, (2, 0, 1, 3)).reshape(kernel.shape[2], -1)


def shards(
    source,
    fetch_blocks,
    pixel_cells,
    pixel_weights,
    seam_flip,
    encode_weight,
    encode_bias,
    first_kernel,
    first_bias,
    second_kernel,
    second_bias,
):
    wanted = lax.all_to_all(fetch_blocks, ("tile", "sub"), split_axis=2, concat_axis=1, tiled=True)
    slots, devices = wanted.shape[0], wanted.shape[1]
    chosen = project_blocks(source, wanted.reshape(-1), encode_weight)
    chosen = chosen.reshape((slots, devices) + chosen.shape[1:])
    arrived = lax.all_to_all(chosen, ("tile", "sub"), split_axis=1, concat_axis=1, tiled=True)
    blocks = arrived.reshape((-1,) + arrived.shape[2:])
    encoded, edges = lookup(blocks, pixel_cells, pixel_weights, encode_bias)
    hidden, hidden_edges = conv(
        encoded, halos(encoded, edges, seam_flip), kernel_matrix(first_kernel), first_bias
    )
    features = conv(
        hidden,
        halos(hidden, hidden_edges, seam_flip),
        kernel_matrix(second_kernel),
        second_bias,
        encoded,
    )
    return jnp.transpose(features, (1, 0, 2))


def solution(mesh):
    in_specs = (
        P(("tile", "sub"), None),
        P(None, ("tile", "sub"), None),
        P(None, ("tile", "sub"), None),
        P(None, ("tile", "sub"), None),
        P(),
        P(),
        P(),
        P(),
        P(),
        P(),
        P(),
    )
    out_specs = P(None, ("tile", "sub"), None)
    return jax.shard_map(shards, mesh=mesh, in_specs=in_specs, out_specs=out_specs, check_vma=False)
```
